32 devices in a mesh: row: 4 (over z), col: 2 (over core), rep: 4 (over y, x).
Axes of the slice: x: 2, y: 2, z: 4, core: 2. Of those that a mesh axis runs over, the one named last changes fastest.
Arguments:
- pre_act: bfloat16 [16384, 12288], P(('rep', 'col'), 'row'), may hold values from -8 to 8
- w_out: bfloat16 [12288, 6144], P('row', 'col'), may hold values from -0.0546875 to 0.0546875
- grad_out: bfloat16 [16384, 6144], P(('rep', 'row'), 'col'), may hold values from -6 to 6
Outputs:
- grad_pre: bfloat16 [16384, 12288], P(('rep', 'col'), 'row')
- grad_weight: float32 [12288, 6144], P(('row', 'rep'), 'col')
The draws below stay inside these ranges and needn't reach their ends.
All inputs are finite; a program needn't handle non-finite values.
Results may differ from the reference program's by a relative error of at most 0.0027.
Values may be sent and summed in bfloat16 or wider, within the bound.
No kernel may reach another device: no remote copies, remote signals or barrier semaphores. Data moves between devices by JAX's collectives and lax.ppermute only.
A program may use at most 256 MiB of HBM per device.

```python
import jax
import jax.numpy as jnp

D = 6144
FW = 12288
TOKENS = 16384


def level_of(key, extent, shards, least, top_value):
    gain, own = 1.0, jax.random.fold_in(key, 6)
    for axis_at, parts in shards:
        heights = jnp.exp(jax.random.uniform(jax.random.fold_in(own, axis_at), (parts,), jnp.float32, least / len(shards), top_value / len(shards)))
        gain = gain * jnp.repeat(heights, extent[axis_at] // parts).reshape([-1 if axis == axis_at else 1 for axis in range(len(extent))])
    return gain


def scatter_about(stream_key, shape, scale, limit, cuts=(), dtype=jnp.bfloat16):
    values = jax.random.normal(stream_key, shape, jnp.float32) * scale
    if len(cuts) > 0:
        values = level_of(stream_key, shape, cuts, -0.22, 0.18) * values
    return jnp.clip(values, min=-limit, max=limit).astype(dtype)


def setup_inputs(seed: int = 0) -> dict:
    splits = jax.random.split(jax.random.key(seed), 4)
    return {
        "pre_act": scatter_about(splits[0], (TOKENS, FW), 1.5, 8.0, ((0, 8), (1, 4))),
        "w_out": scatter_about(splits[1], (FW, D), FW ** -0.5, 0.0546875, ((0, 4), (1, 2))),
        "grad_out": scatter_about(splits[2], (TOKENS, D), 1.0, 6.0, ((0, 16), (1, 2))),
    }


SQRT_TWO_PI = 0.7978845608028654
CUBIC = 0.044715


def gelu_pair(values):
    inner = SQRT_TWO_PI * (values + CUBIC * values * values * values)
    bent = jnp.tanh(inner)
    output = 0.5 * values * (1.0 + bent)
    slopes = 0.5 * (1.0 + bent) + 0.5 * values * (1.0 - bent * bent) * SQRT_TWO_PI * (1.0 + 3.0 * CUBIC * values * values)
    return output, slopes


def reference(pre_act, w_out, grad_out):
    output, slopes = gelu_pair(pre_act.astype(jnp.float32))
    activation = output.astype(jnp.bfloat16)
    grad_act = jnp.dot(grad_out, w_out.T, preferred_element_type=jnp.float32)
    grad_pre = (grad_act * slopes).astype(jnp.bfloat16)
    grad_weight = jnp.dot(activation.T, grad_out, preferred_element_type=jnp.float32) * (TOKENS ** -0.5)
    return grad_pre, grad_weight
```

```python
import jax
import jax.numpy as jnp
from jax import lax
from jax.sharding import PartitionSpec as P

SQRT_TWO_PI = 0.7978845608028654
CUBIC = 0.044715
WINDOW = 3
RING_LIMIT = 8


def gelu(values):
    inner = SQRT_TWO_PI * (values + CUBIC * values * values * values)
    return 0.5 * values * (1.0 + jnp.tanh(inner))


def gelu_slopes(values):
    inner = SQRT_TWO_PI * (values + CUBIC * values * values * values)
    bent = jnp.tanh(inner)
    return 0.5 * (1.0 + bent) + 0.5 * values * (1.0 - bent * bent) * SQRT_TWO_PI * (
        1.0 + 3.0 * CUBIC * values * values
    )


def contract_rows(left, right):
    return lax.dot_general(
        left, right, (((0,), (0,)), ((), ())), preferred_element_type=jnp.float32
    )


def contract_columns(left, right):
    return lax.dot_general(
        left, right, (((1,), (1,)), ((), ())), preferred_element_type=jnp.float32
    )


def chunk_widths(width):
    unit = 128
    for parts in (12, 8, 6, 4):
        if width % (parts * unit) == 0:
            unit = width // parts
            return [2 * unit] * (parts // 2 - 1) + [unit, unit]
    return [width]


def meet(one, other):
    return lax.optimization_barrier((one, other))[0]


def swap(x, axis, size, step):
    return lax.ppermute(x, axis, [(i, (i + step) % size) for i in range(size)])


def gather_rows(chunks, n, nc):
    row, col = lax.axis_index("row"), lax.axis_index("col")
    shift = col * (n // nc)
    count, rows = len(chunks), chunks[0].shape[0]

    if n > RING_LIMIT:
        out = []
        for chunk in chunks:
            whole = lax.all_gather(chunk, "row", axis=0, tiled=True)
            twice = jnp.concatenate([whole, whole], axis=0)
            out.append(lax.dynamic_slice_in_dim(twice, shift * rows, n * rows, 0))
        return out

    def place(buffer, piece, step):
        slot = (row - step + 2 * n - shift) % n
        return lax.dynamic_update_slice_in_dim(buffer, piece, slot * rows, 0)

    order = [
        (t - s, s) for t in range(count + n - 2) for s in range(n - 1) if 0 <= t - s < count
    ]
    held = list(chunks)
    buffers = [
        place(jnp.zeros((n * rows, c.shape[1]), c.dtype), c, 0) for c in chunks
    ]
    done = []
    for index, (k, s) in enumerate(order):
        source = held[k]
        if index >= WINDOW:
            source = meet(source, done[index - WINDOW])
        held[k] = swap(source, "row", n, 1)
        done.append(held[k])
        buffers[k] = place(buffers[k], held[k], s + 1)
    return buffers


def solution(mesh):
    n, nc, nr = (mesh.shape[axis] for axis in ("row", "col", "rep"))
    pairs = nr & (nr - 1) == 0

    def partner(p, d):
        return p ^ d if pairs else (p + d) % nr

    def on_device(pre_act, w_out, grad_out):
        tokens = grad_out.shape[0] * n * nr
        factor = float(tokens) ** (-0.5)
        rep = lax.axis_index("rep")
        mine_rows, hidden = pre_act.shape
        part = hidden // nr
        widths = chunk_widths(grad_out.shape[1])
        starts = [sum(widths[:k]) for k in range(len(widths))]
        spans = [slice(a, a + b) for a, b in zip(starts, widths)]

        gathered = gather_rows([grad_out[:, span] for span in spans], n, nc)

        acts = []
        for d in range(nr):
            block = lax.dynamic_slice_in_dim(pre_act, partner(rep, d) * part, part, 1)
            own = gelu(block.astype(jnp.float32)).astype(jnp.bfloat16)
            rest = [swap(own, "col", nc, nc - j) for j in range(1, nc)]
            acts.append(jnp.concatenate([own] + rest, axis=0))
        weights = [w_out] + [swap(w_out, "col", nc, nc - j) for j in range(1, nc)]

        grad_act = None
        grad_weight = jnp.zeros((part, grad_out.shape[1]), jnp.float32)
        slopes = gelu_slopes(pre_act.astype(jnp.float32))
        for span, block in zip(spans, gathered):
            features = [block[:mine_rows]]
            for j in range(1, nc):
                other = block[j * mine_rows : (j + 1) * mine_rows]
                features.append(swap(other, "col", nc, j))
            total = None
            arrived = []
            for d in range(nr - 1, 0, -1):
                term = (contract_rows(acts[d], block) * factor).astype(jnp.bfloat16)
                pairs_d = [(p, partner(p, d)) for p in range(nr)]
                arrived.append(lax.ppermute(term, "rep", pairs_d))
            total = contract_rows(acts[0], block) * factor
            left = jnp.concatenate(features, axis=1)
            right = jnp.concatenate([w[:, span] for w in weights], axis=1)
            term = contract_columns(left, right)
            grad_act = term if grad_act is None else grad_act + term
            for other in arrived:
                total = total + other.astype(jnp.float32)
            grad_weight = lax.dynamic_update_slice_in_dim(grad_weight, total, span.start, 1)
        grad_pre = (grad_act * slopes).astype(jnp.bfloat16)
        return grad_pre, grad_weight

    in_specs = (P(("rep", "col"), "row"), P("row", "col"), P(("rep", "row"), "col"))
    out_specs = (P(("rep", "col"), "row"), P(("row", "rep"), "col"))
    return jax.shard_map(
        on_device, mesh=mesh, in_specs=in_specs, out_specs=out_specs, check_vma=False
    )
```

```python
import functools

import jax
import jax.numpy as jnp
from jax import lax
from jax.experimental import pallas as pl
from jax.experimental.pallas import tpu as pltpu
from jax.sharding import PartitionSpec as P

SQRT_TWO_PI = 0.7978845608028654
CUBIC = 0.044715
VMEM_LIMIT = 56 * 1024 * 1024
BLOCK = 768
SHARES = 24
STAGES = ((10, 0), (8, 16), (4, 12), (2, 10))

ANY = pl.BlockSpec(memory_space=pl.ANY)
TOKEN = jax.ShapeDtypeStruct((8, 128), jnp.float32)
FREE = pl.CostEstimate(flops=0, bytes_accessed=0, transcendentals=0)


def gelu_pair(x):
    square = x * x
    bent = jnp.tanh(x * (SQRT_TWO_PI + (SQRT_TWO_PI * CUBIC) * square))
    rise = x * (SQRT_TWO_PI + (3.0 * SQRT_TWO_PI * CUBIC) * square)
    up = 0.5 + 0.5 * bent
    return x * up, up + rise * (0.5 - 0.5 * (bent * bent))


def params():
    return pltpu.CompilerParams(vmem_limit_bytes=VMEM_LIMIT)


def divisor(size, most, unit):
    for block in range(most - most % unit, 0, -unit):
        if size % block == 0:
            return block
    return size


def stages_of(width):
    if width % (SHARES * 128) == 0:
        share = width // SHARES
        return [(w * share, at * share) for w, at in STAGES]
    return [(width, 0)]


def swap(x, axis, size, step):
    return lax.ppermute(x, axis, [(i, (i + step) % size) for i in range(size)])


def cut(token, array, width, first):
    rows = array.shape[0]
    tall = divisor(rows, 256, 16)

    def kernel(array_ref, token_ref, out_ref, token_out):
        out_ref[...] = array_ref[...]

    out = pl.pallas_call(
        kernel,
        out_shape=[jax.ShapeDtypeStruct((rows, width), array.dtype), TOKEN],
        grid=(rows // tall,),
        in_specs=[pl.BlockSpec((tall, width), lambda i: (i, first // width)), ANY],
        out_specs=[pl.BlockSpec((tall, width), lambda i: (i, 0)), ANY],
        cost_estimate=FREE,
        compiler_params=params(),
    )(array, token)
    return out[1], out[0]


def activate(token, pre_act):
    rows, hidden = pre_act.shape
    tall, wide = divisor(rows, 512, 128), divisor(hidden, 512, 128)

    def kernel(x_ref, token_ref, out_ref, slopes_ref, token_out):
        value, slopes = gelu_pair(x_ref[...].astype(jnp.float32))
        out_ref[...] = value.T.astype(jnp.bfloat16)
        slopes_ref[...] = slopes

    tile = pl.BlockSpec((tall, wide), lambda j, i: (i, j))
    out = pl.pallas_call(
        kernel,
        out_shape=[
            jax.ShapeDtypeStruct((hidden, rows), jnp.bfloat16),
            jax.ShapeDtypeStruct((rows, hidden), jnp.float32),
            TOKEN,
        ],
        grid=(hidden // wide, rows // tall),
        in_specs=[tile, ANY],
        out_specs=[pl.BlockSpec((wide, tall), lambda j, i: (j, i)), tile, ANY],
        cost_estimate=FREE,
        compiler_params=params(),
    )(pre_act, token)
    return out[2], out[0], out[1]


def terms(token, table, pieces, acts, part, group, send, factor, with_rows):
    nc, rows, width = len(acts), acts[0].shape[1], pieces[0][0].shape[1]
    hidden = acts[0].shape[0]
    block = divisor(part, BLOCK if width <= 1024 else BLOCK // 2, 16)
    blocks = part // block
    base = len(pieces)
    steps = len(group) * blocks
    away = (len(group) - group.count(0)) * blocks
    own = group[-1] == 0
    strip = rows // steps if with_rows else 0

    def kernel(table_ref, *refs):
        refs = list(refs)
        piece_refs = [refs.pop(0) for _ in pieces]
        act_refs = [refs.pop(0) for _ in acts]
        refs.pop(0)
        if send is not None:
            refs.pop(0)
        send_ref = refs.pop(0) if away else None
        own_ref = refs.pop(0) if own else None
        row_outs = [refs.pop(0) for _ in range(nc if with_rows else 0)]
        refs.pop(0)
        held, sems = refs
        i = pl.program_id(0)

        @pl.when(i == 0)
        def _():
            copies = []
            for p, (_, first, count, place) in enumerate(pieces):
                to = pl.multiple_of(table_ref[place], 16)
                copies.append(
                    pltpu.make_async_copy(
                        piece_refs[p].at[pl.ds(first, count)], held.at[pl.ds(to, count)], sems.at[p]
                    )
                )
            for copy in copies:
                copy.start()
            for copy in copies:
                copy.wait()

        for j, ref in enumerate(row_outs):
            ref[...] = held[pl.ds(pl.multiple_of(j * rows + i * strip, 16), strip), :]
        total = None
        for j in range(nc):
            term = jnp.dot(
                act_refs[j][...],
                held[j * rows : (j + 1) * rows, :],
                preferred_element_type=jnp.float32,
            )
            total = term if total is None else total + term
        total = total * factor
        if away and own:

            @pl.when(i < away)
            def _():
                send_ref[...] = total.astype(send_ref.dtype)

            @pl.when(i >= away)
            def _():
                own_ref[...] = total

        elif own:
            own_ref[...] = total
        else:
            send_ref[...] = total.astype(send_ref.dtype)

    def act_map(i, table_ref):
        distance = group[0] - i // blocks
        return table_ref[base + distance] * blocks + i % blocks, 0

    def send_map(i, table_ref):
        return act_map(jnp.minimum(i, away - 1), table_ref)

    shapes, specs, aliases = [], [], {}
    operands = [p[0] for p in pieces] + list(acts) + [token]
    in_specs = [ANY] * len(pieces) + [pl.BlockSpec((block, rows), act_map)] * nc + [ANY]
    if send is not None:
        operands.append(send)
        in_specs.append(ANY)
        if away:
            aliases = {len(operands): 0}
    if away:
        shapes.append(jax.ShapeDtypeStruct((hidden, width), jnp.bfloat16))
        specs.append(pl.BlockSpec((block, width), send_map))
    if own:
        shapes.append(jax.ShapeDtypeStruct((part, width), jnp.float32))
        specs.append(
            pl.BlockSpec((block, width), lambda i, t: (jnp.clip(i - away, 0, blocks - 1), 0))
        )
    if with_rows:
        shapes += [jax.ShapeDtypeStruct((rows, width), jnp.bfloat16)] * nc
        specs += [pl.BlockSpec((strip, width), lambda i, t: (i, 0))] * nc
    out = list(
        pl.pallas_call(
            kernel,
            out_shape=shapes + [TOKEN],
            grid_spec=pltpu.PrefetchScalarGridSpec(
                num_scalar_prefetch=1,
                grid=(steps,),
                in_specs=in_specs,
                out_specs=specs + [ANY],
                scratch_shapes=[
                    pltpu.VMEM((nc * rows, width), jnp.bfloat16),
                    pltpu.SemaphoreType.DMA((len(pieces),)),
                ],
            ),
            input_output_aliases=aliases,
            cost_estimate=FREE,
            compiler_params=params(),
        )(table, *operands)
    )
    sent = out.pop(0) if away else send
    kept = out.pop(0) if own else None
    return out[-1], sent, kept, out[:-1]


def products(token, features, weights, span, total, slopes):
    width, first = span
    rows, hidden = features[0].shape[0], weights[0].shape[0]
    nc = len(weights)
    last = slopes is not None
    tall = divisor(rows, 512 if nc * width <= 1024 else 256, 16)

    def kernel(*refs):
        refs = list(refs)
        lefts = [refs.pop(0) for _ in range(nc)]
        rights = [refs.pop(0) for _ in range(nc)]
        total_ref = refs.pop(0) if total is not None else None
        slopes_ref = refs.pop(0) if last else None
        out_ref = refs[1]
        value = None
        for left, right in zip(lefts, rights):
            term = lax.dot_general(
                left[...],
                right[...],
                (((1,), (1,)), ((), ())),
                preferred_element_type=jnp.float32,
            )
            value = term if value is None else value + term
        if total_ref is not None:
            value = value + total_ref[...]
        if last:
            value = value * slopes_ref[...]
        out_ref[...] = value.astype(out_ref.dtype)

    tile = pl.BlockSpec((tall, hidden), lambda i: (i, 0))
    operands = list(features) + list(weights)
    specs = [pl.BlockSpec((tall, width), lambda i: (i, 0))] * nc
    specs += [
        pl.BlockSpec(
            (hidden, width), lambda i: (0, first // width), pipeline_mode=pl.Buffered(1)
        )
    ] * nc
    aliases = {}
    if total is not None:
        if not last:
            aliases = {len(operands): 0}
        operands.append(total)
        specs.append(tile)
    if last:
        operands.append(slopes)
        specs.append(tile)
    kind = jnp.bfloat16 if last else jnp.float32
    out = pl.pallas_call(
        kernel,
        out_shape=[jax.ShapeDtypeStruct((rows, hidden), kind), TOKEN],
        grid=(rows // tall,),
        in_specs=specs + [ANY],
        out_specs=[tile, ANY],
        input_output_aliases=aliases,
        cost_estimate=FREE,
        compiler_params=params(),
    )(*operands, token)
    return out[1], out[0]


def add_up(token, table, base, own, arrived, whole, shape, span):
    width, first = span
    rows = shape[0]
    tall = divisor(rows, 384, 16)
    steps = rows // tall
    count = arrived.shape[0] // rows - 1

    def kernel(table_ref, *refs):
        value = refs[0][...]
        for ref in refs[1 : 1 + count]:
            value = value + ref[...].astype(jnp.float32)
        refs[-2][...] = value

    def other(d):
        return pl.BlockSpec((tall, width), lambda i, t: (t[base + d] * steps + i, 0))

    operands = [own] + [arrived] * count
    specs, aliases = [pl.BlockSpec((tall, width), lambda i, t: (i, 0))], {}
    specs += [other(d) for d in range(1, count + 1)]
    if whole is not None:
        aliases = {len(operands) + 1: 0}
        operands.append(whole)
        specs.append(ANY)
    out = pl.pallas_call(
        kernel,
        out_shape=[jax.ShapeDtypeStruct(shape, jnp.float32), TOKEN],
        grid_spec=pltpu.PrefetchScalarGridSpec(
            num_scalar_prefetch=1,
            grid=(steps,),
            in_specs=specs + [ANY],
            out_specs=[pl.BlockSpec((tall, width), lambda i, t: (i, first // width)), ANY],
        ),
        input_output_aliases=aliases,
        cost_estimate=FREE,
        compiler_params=params(),
    )(table, *operands, token)
    return out[1], out[0]


def on_device(n, nc, nr, pre_act, w_out, grad_out):
    tokens = grad_out.shape[0] * n * nr
    factor = float(tokens) ** (-0.5)
    col, rep = lax.axis_index("col"), lax.axis_index("rep")
    rows, hidden = pre_act.shape
    part = hidden // nr
    shape = (part, grad_out.shape[1])
    spans = stages_of(grad_out.shape[1])
    count = len(spans)
    distances = list(range(nr - 1, -1, -1))

    def partner(d):
        return rep ^ d if nr & (nr - 1) == 0 else (rep + d) % nr

    places = [((j - col + nc) % nc) * rows for j in range(nc)]
    table = jnp.stack([jnp.int32(v) for v in places + [partner(d) for d in range(nr)]])
    token = jnp.zeros(TOKEN.shape, TOKEN.dtype)
    gathered, features, owns, arrived = {}, {}, {}, {}
    grad_act = grad_weight = None

    def gather(token, k):
        if k >= count:
            return token
        token, columns = cut(token, grad_out, *spans[k])
        gathered[k] = lax.all_gather(columns, "row", axis=0, tiled=True)
        return token

    token = gather(token, 0)
    token = gather(token, 1)
    token, act, slopes = activate(token, pre_act)
    acts = [act] + [swap(act, "col", nc, nc - j) for j in range(1, nc)]
    weights = [w_out] + [swap(w_out, "col", nc, nc - j) for j in range(1, nc)]
    token = gather(token, 2)

    for k in range(count):
        listed = [(gathered[k], j * rows, rows, j) for j in range(nc)]
        token, sent, own, own_rows = terms(
            token, table, listed, acts, part, distances, None, factor, True
        )
        features[k] = [own_rows[0]] + [swap(own_rows[j], "col", nc, j) for j in range(1, nc)]
        owns[k] = arrived[k] = own
        if nr > 1:
            arrived[k] = lax.all_to_all(sent, "rep", 0, 0, tiled=True)
        token = gather(token, k + 3)
        if k > 0:
            token, grad_weight = add_up(
                token, table, nc, owns[k - 1], arrived[k - 1], grad_weight, shape, spans[k - 1]
            )
        token, grad_act = products(
            token, features[k], weights, spans[k], grad_act, slopes if k == count - 1 else None
        )
    token, grad_weight = add_up(
        token, table, nc, owns[count - 1], arrived[count - 1], grad_weight, shape, spans[count - 1]
    )
    return grad_act, grad_weight


def solution(mesh):
    n, nc, nr = (mesh.shape[axis] for axis in ("row", "col", "rep"))
    in_specs = (P(("rep", "col"), "row"), P("row", "col"), P(("rep", "row"), "col"))
    out_specs = (P(("rep", "col"), "row"), P(("row", "rep"), "col"))
    return jax.shard_map(
        functools.partial(on_device, n, nc, nr),
        mesh=mesh,
        in_specs=in_specs,
        out_specs=out_specs,
        check_vma=False,
    )
```

```python
import functools

import jax
import jax.numpy as jnp
from jax import lax
from jax.experimental import pallas as pl
from jax.experimental.pallas import tpu as pltpu
from jax.sharding import PartitionSpec as P

SQRT_TWO_PI = 0.7978845608028654
CUBIC = 0.044715
VMEM_LIMIT = 56 * 1024 * 1024
BLOCK = 768
SHARES = 24
STAGES = ((2, 10), (10, 0), (8, 16), (4, 12))
RING_LIMIT = 8
PERMUTED, LATE = 1, 1
GROUPS = ((0,), (1,), (2,), (3,))

ANY = pl.BlockSpec(memory_space=pl.ANY)
TOKEN = jax.ShapeDtypeStruct((8, 128), jnp.float32)
FREE = pl.CostEstimate(flops=0, bytes_accessed=0, transcendentals=0)


def gelu_pair(x):
    square = x * x
    bent = jnp.tanh(x * (SQRT_TWO_PI + (SQRT_TWO_PI * CUBIC) * square))
    rise = x * (SQRT_TWO_PI + (3.0 * SQRT_TWO_PI * CUBIC) * square)
    up = 0.5 + 0.5 * bent
    return x * up, up + rise * (0.5 - 0.5 * (bent * bent))


def params():
    return pltpu.CompilerParams(vmem_limit_bytes=VMEM_LIMIT)


def divisor(size, most, unit):
    for block in range(most - most % unit, 0, -unit):
        if size % block == 0:
            return block
    return size


def stages_of(width):
    if width % (SHARES * 128) == 0:
        share = width // SHARES
        return [(w * share, at * share) for w, at in STAGES]
    return [(width, 0)]


def swap(x, axis, size, step):
    return lax.ppermute(x, axis, [(i, (i + step) % size) for i in range(size)])


def pass_on(token, array):
    def kernel(*refs):
        pass

    out = pl.pallas_call(
        kernel,
        out_shape=[jax.ShapeDtypeStruct(array.shape, array.dtype), TOKEN],
        in_specs=[ANY] * 2,
        out_specs=[ANY] * 2,
        input_output_aliases={0: 0},
        cost_estimate=FREE,
        compiler_params=params(),
    )(array, token)
    return out[1], out[0]


def cut(token, array, width, first):
    rows = array.shape[0]
    tall = divisor(rows, 256, 16)

    def kernel(array_ref, token_ref, out_ref, token_out):
        out_ref[...] = array_ref[...]

    out = pl.pallas_call(
        kernel,
        out_shape=[jax.ShapeDtypeStruct((rows, width), array.dtype), TOKEN],
        grid=(rows // tall,),
        in_specs=[pl.BlockSpec((tall, width), lambda i: (i, first // width)), ANY],
        out_specs=[pl.BlockSpec((tall, width), lambda i: (i, 0)), ANY],
        cost_estimate=FREE,
        compiler_params=params(),
    )(array, token)
    return out[1], out[0]


def activate(token, pre_act):
    rows, hidden = pre_act.shape
    tall, wide = divisor(rows, 512, 128), divisor(hidden, 512, 128)

    def kernel(x_ref, token_ref, out_ref, slopes_ref, token_out):
        value, slopes = gelu_pair(x_ref[...].astype(jnp.float32))
        out_ref[...] = value.T.astype(jnp.bfloat16)
        slopes_ref[...] = slopes

    tile = pl.BlockSpec((tall, wide), lambda j, i: (i, j))
    out = pl.pallas_call(
        kernel,
        out_shape=[
            jax.ShapeDtypeStruct((hidden, rows), jnp.bfloat16),
            jax.ShapeDtypeStruct((rows, hidden), jnp.float32),
            TOKEN,
        ],
        grid=(hidden // wide, rows // tall),
        in_specs=[tile, ANY],
        out_specs=[pl.BlockSpec((wide, tall), lambda j, i: (j, i)), tile, ANY],
        cost_estimate=FREE,
        compiler_params=params(),
    )(pre_act, token)
    return out[2], out[0], out[1]


def terms(token, table, base, pieces, acts, part, group, send, factor, with_rows):
    nc, rows, width = len(acts), acts[0].shape[1], pieces[0][0].shape[1]
    hidden = acts[0].shape[0]
    block = divisor(part, BLOCK if width <= 1024 else BLOCK // 2, 16)
    blocks = part // block
    steps = len(group) * blocks
    away = (len(group) - group.count(0)) * blocks
    own = group[-1] == 0
    strip = rows // steps if with_rows else 0

    def kernel(table_ref, *refs):
        refs = list(refs)
        piece_refs = [refs.pop(0) for _ in pieces]
        act_refs = [refs.pop(0) for _ in acts]
        refs.pop(0)
        if send is not None:
            refs.pop(0)
        send_ref = refs.pop(0) if away else None
        own_ref = refs.pop(0) if own else None
        row_outs = [refs.pop(0) for _ in range(nc if with_rows else 0)]
        refs.pop(0)
        held, sems = refs
        i = pl.program_id(0)

        @pl.when(i == 0)
        def _():
            copies = []
            for p, (_, first, count, place) in enumerate(pieces):
                to = pl.multiple_of(table_ref[place], 16)
                copies.append(
                    pltpu.make_async_copy(
                        piece_refs[p].at[pl.ds(first, count)], held.at[pl.ds(to, count)], sems.at[p]
                    )
                )
            for copy in copies:
                copy.start()
            for copy in copies:
                copy.wait()

        for j, ref in enumerate(row_outs):
            ref[...] = held[pl.ds(pl.multiple_of(j * rows + i * strip, 16), strip), :]
        total = None
        for j in range(nc):
            term = jnp.dot(
                act_refs[j][...],
                held[j * rows : (j + 1) * rows, :],
                preferred_element_type=jnp.float32,
            )
            total = term if total is None else total + term
        total = total * factor
        if away and own:

            @pl.when(i < away)
            def _():
                send_ref[...] = total.astype(send_ref.dtype)

            @pl.when(i >= away)
            def _():
                own_ref[...] = total

        elif own:
            own_ref[...] = total
        else:
            send_ref[...] = total.astype(send_ref.dtype)

    def act_map(i, table_ref):
        distance = group[0] - i // blocks
        return table_ref[base + distance] * blocks + i % blocks, 0

    def send_map(i, table_ref):
        return act_map(jnp.minimum(i, away - 1), table_ref)

    shapes, specs, aliases = [], [], {}
    operands = [p[0] for p in pieces] + list(acts) + [token]
    in_specs = [ANY] * len(pieces) + [pl.BlockSpec((block, rows), act_map)] * nc + [ANY]
    if send is not None:
        operands.append(send)
        in_specs.append(ANY)
        if away:
            aliases = {len(operands): 0}
    if away:
        shapes.append(jax.ShapeDtypeStruct((hidden, width), jnp.bfloat16))
        specs.append(pl.BlockSpec((block, width), send_map))
    if own:
        shapes.append(jax.ShapeDtypeStruct((part, width), jnp.float32))
        specs.append(
            pl.BlockSpec((block, width), lambda i, t: (jnp.clip(i - away, 0, blocks - 1), 0))
        )
    if with_rows:
        shapes += [jax.ShapeDtypeStruct((rows, width), jnp.bfloat16)] * nc
        specs += [pl.BlockSpec((strip, width), lambda i, t: (i, 0))] * nc
    out = list(
        pl.pallas_call(
            kernel,
            out_shape=shapes + [TOKEN],
            grid_spec=pltpu.PrefetchScalarGridSpec(
                num_scalar_prefetch=1,
                grid=(steps,),
                in_specs=in_specs,
                out_specs=specs + [ANY],
                scratch_shapes=[
                    pltpu.VMEM((nc * rows, width), jnp.bfloat16),
                    pltpu.SemaphoreType.DMA((len(pieces),)),
                ],
            ),
            input_output_aliases=aliases,
            cost_estimate=FREE,
            compiler_params=params(),
        )(table, *operands)
    )
    sent = out.pop(0) if away else send
    kept = out.pop(0) if own else None
    return out[-1], sent, kept, out[:-1]


def products(token, features, weights, spans, total, slopes):
    rows, hidden = features[0][0].shape[0], weights[0].shape[0]
    nc = len(weights)
    last = slopes is not None
    wide = nc * sum(width for width, _ in spans)
    tall = divisor(rows, 512 if wide <= 1024 else 256, 16)

    def kernel(*refs):
        refs = list(refs)
        lefts = [refs.pop(0) for _ in range(nc * len(spans))]
        rights = [refs.pop(0) for _ in range(nc * len(spans))]
        total_ref = refs.pop(0) if total is not None else None
        slopes_ref = refs.pop(0) if last else None
        out_ref = refs[1]
        value = None
        for left, right in zip(lefts, rights):
            term = lax.dot_general(
                left[...],
                right[...],
                (((1,), (1,)), ((), ())),
                preferred_element_type=jnp.float32,
            )
            value = term if value is None else value + term
        if total_ref is not None:
            value = value + total_ref[...]
        if last:
            value = value * slopes_ref[...]
        out_ref[...] = value.astype(out_ref.dtype)

    tile = pl.BlockSpec((tall, hidden), lambda i: (i, 0))
    operands, specs = [], []
    for ours, (width, _) in zip(features, spans):
        operands += ours
        specs += [pl.BlockSpec((tall, width), lambda i: (i, 0))] * nc
    for width, first in spans:
        operands += weights
        specs += [
            pl.BlockSpec(
                (hidden, width),
                lambda i, b=first // width: (0, b),
                pipeline_mode=pl.Buffered(1),
            )
        ] * nc
    aliases = {}
    if total is not None:
        if not last:
            aliases = {len(operands): 0}
        operands.append(total)
        specs.append(tile)
    if last:
        operands.append(slopes)
        specs.append(tile)
    kind = jnp.bfloat16 if last else jnp.float32
    out = pl.pallas_call(
        kernel,
        out_shape=[jax.ShapeDtypeStruct((rows, hidden), kind), TOKEN],
        grid=(rows // tall,),
        in_specs=specs + [ANY],
        out_specs=[tile, ANY],
        input_output_aliases=aliases,
        cost_estimate=FREE,
        compiler_params=params(),
    )(*operands, token)
    return out[1], out[0]


def add_up(token, table, base, own, arrived, whole, shape, span):
    width, first = span
    rows = shape[0]
    tall = divisor(rows, 384, 16)
    steps = rows // tall
    whole_blocks = len(arrived) == 1 and arrived[0].shape[0] > rows
    count = arrived[0].shape[0] // rows - 1 if whole_blocks else len(arrived)

    def kernel(table_ref, *refs):
        value = refs[0][...]
        for ref in refs[1 : 1 + count]:
            value = value + ref[...].astype(jnp.float32)
        refs[-2][...] = value

    def other(d):
        if not whole_blocks:
            return pl.BlockSpec((tall, width), lambda i, t: (i, 0))
        return pl.BlockSpec((tall, width), lambda i, t: (t[base + d] * steps + i, 0))

    operands = [own] + (arrived * count if whole_blocks else arrived)
    specs, aliases = [pl.BlockSpec((tall, width), lambda i, t: (i, 0))], {}
    specs += [other(d) for d in range(1, count + 1)]
    if whole is not None:
        aliases = {len(operands) + 1: 0}
        operands.append(whole)
        specs.append(ANY)
    out = pl.pallas_call(
        kernel,
        out_shape=[jax.ShapeDtypeStruct(shape, jnp.float32), TOKEN],
        grid_spec=pltpu.PrefetchScalarGridSpec(
            num_scalar_prefetch=1,
            grid=(steps,),
            in_specs=specs + [ANY],
            out_specs=[pl.BlockSpec((tall, width), lambda i, t: (i, first // width)), ANY],
        ),
        input_output_aliases=aliases,
        cost_estimate=FREE,
        compiler_params=params(),
    )(table, *operands, token)
    return out[1], out[0]


def on_device(n, nc, nr, pre_act, w_out, grad_out):
    tokens = grad_out.shape[0] * n * nr
    factor = float(tokens) ** (-0.5)
    row, col, rep = (lax.axis_index(axis) for axis in ("row", "col", "rep"))
    local = grad_out.shape[0]
    rows, hidden = pre_act.shape
    part = hidden // nr
    shape = (part, grad_out.shape[1])
    spans = stages_of(grad_out.shape[1])
    count = len(spans)
    groups = GROUPS if count == len(STAGES) else ((0,),)
    distances = list(range(nr - 1, -1, -1))

    def partner(d):
        return rep ^ d if nr & (nr - 1) == 0 else (rep + d) % nr

    places = [((j - col + nc) % nc) * rows for j in range(nc)]
    ring = n <= RING_LIMIT and n % nc == 0 and count > 1
    slots = [(row - s + 2 * n - col * (n // nc)) % n * local for s in range(n if ring else 0)]
    partners = [partner(d) for d in range(nr)]
    table = jnp.stack([jnp.int32(v) for v in places + partners + slots])
    token = jnp.zeros(TOKEN.shape, TOKEN.dtype)
    gathered, features, owns, arrived = {}, {}, {}, {}
    grad_act = grad_weight = None

    def gather(token, k):
        if k >= count:
            return token
        token, columns = cut(token, grad_out, *spans[k])
        gathered[k] = lax.all_gather(columns, "row", axis=0, tiled=True)
        return token

    def add_stage(token, k, whole):
        return add_up(token, table, nc, owns[k], arrived[k], whole, shape, spans[k])

    steps = []
    token = gather(token, 1 if ring else 0)
    if ring:
        token, columns = cut(token, grad_out, *spans[0])
        steps = [columns]
    token = gather(token, 2 if ring else 1)
    token, act, slopes = activate(token, pre_act)
    acts = [act] + [swap(act, "col", nc, nc - j) for j in range(1, nc)]
    weights = [w_out] + [swap(w_out, "col", nc, nc - j) for j in range(1, nc)]
    for s in range(1, n if ring else 0):
        piece = swap(steps[-1], "row", n, 1)
        if s < n - 1:
            token, piece = pass_on(token, piece)
        steps.append(piece)
    if not ring:
        token = gather(token, 2)

    for k in range(count):
        if 0 < k < count - LATE:
            token, grad_weight = add_stage(token, k - 1, grad_weight)
        if ring and k == 0:
            listed = [(steps[s], 0, local, nc + nr + s) for s in range(n)]
        else:
            listed = [(gathered[k], j * rows, rows, j) for j in range(nc)]
        token, sent, own, own_rows = terms(
            token, table, nc, listed, acts, part, distances, None, factor, True
        )
        features[k] = [own_rows[0]] + [swap(own_rows[j], "col", nc, j) for j in range(1, nc)]
        owns[k], arrived[k] = own, []
        if nr > 1 and k < max(1, count - PERMUTED):
            arrived[k] = [lax.all_to_all(sent, "rep", 0, 0, tiled=True)]
        elif nr > 1:
            arrived[k] = []
            for d in distances[:-1]:
                block = lax.dynamic_slice_in_dim(sent, partner(d) * part, part, 0)
                way = [(p, p ^ d if nr & (nr - 1) == 0 else (p + d) % nr) for p in range(nr)]
                arrived[k].append(lax.ppermute(block, "rep", way))
        token = gather(token, k + (2 if ring else 3)) if not ring or k > 0 else token
        for ks in groups:
            if ks[-1] == k:
                token, grad_act = products(
                    token,
                    [features[q] for q in ks],
                    weights,
                    [spans[q] for q in ks],
                    grad_act,
                    slopes if k == count - 1 else None,
                )
    for k in range(max(0, count - LATE - 1), count):
        token, grad_weight = add_stage(token, k, grad_weight)
    return grad_act, grad_weight


def solution(mesh):
    n, nc, nr = (mesh.shape[axis] for axis in ("row", "col", "rep"))
    in_specs = (P(("rep", "col"), "row"), P("row", "col"), P(("rep", "row"), "col"))
    out_specs = (P(("rep", "col"), "row"), P(("row", "rep"), "col"))
    return jax.shard_map(
        functools.partial(on_device, n, nc, nr),
        mesh=mesh,
        in_specs=in_specs,
        out_specs=out_specs,
        check_vma=False,
    )
```

```python
import functools

import jax
import jax.numpy as jnp
from jax import lax
from jax.experimental import pallas as pl
from jax.experimental.pallas import tpu as pltpu
from jax.sharding import PartitionSpec as P

SQRT_TWO_PI = 0.7978845608028654
CUBIC = 0.044715
VMEM_LIMIT = 56 * 1024 * 1024
BLOCK = 768
SHARES = 24
STAGES = ((2, 10), (10, 0), (8, 16), (4, 12))
RING_LIMIT = 8
PERMUTED, LATE = 1, 1
GROUPS = ((0,), (1,), (2,), (3,))

ANY = pl.BlockSpec(memory_space=pl.ANY)
TOKEN = jax.ShapeDtypeStruct((8, 128), jnp.float32)
FREE = pl.CostEstimate(flops=0, bytes_accessed=0, transcendentals=0)


def gelu_pair(x):
    square = x * x
    bent = jnp.tanh(x * (SQRT_TWO_PI + (SQRT_TWO_PI * CUBIC) * square))
    rise = x * (SQRT_TWO_PI + (3.0 * SQRT_TWO_PI * CUBIC) * square)
    up = 0.5 + 0.5 * bent
    return x * up, up + rise * (0.5 - 0.5 * (bent * bent))


def params():
    return pltpu.CompilerParams(vmem_limit_bytes=VMEM_LIMIT)


def divisor(size, most, unit):
    for block in range(most - most % unit, 0, -unit):
        if size % block == 0:
            return block
    return size


def stages_of(width):
    if width % (SHARES * 128) == 0:
        share = width // SHARES
        return [(w * share, at * share) for w, at in STAGES]
    return [(width, 0)]


def swap(x, axis, size, step):
    return lax.ppermute(x, axis, [(i, (i + step) % size) for i in range(size)])


def pass_on(token, array):
    def kernel(*refs):
        pass

    out = pl.pallas_call(
        kernel,
        out_shape=[jax.ShapeDtypeStruct(array.shape, array.dtype), TOKEN],
        in_specs=[ANY] * 2,
        out_specs=[ANY] * 2,
        input_output_aliases={0: 0},
        cost_estimate=FREE,
        compiler_params=params(),
    )(array, token)
    return out[1], out[0]


def cut(token, array, width, first):
    rows = array.shape[0]
    tall = divisor(rows, 256, 16)

    def kernel(array_ref, token_ref, out_ref, token_out):
        out_ref[...] = array_ref[...]

    out = pl.pallas_call(
        kernel,
        out_shape=[jax.ShapeDtypeStruct((rows, width), array.dtype), TOKEN],
        grid=(rows // tall,),
        in_specs=[pl.BlockSpec((tall, width), lambda i: (i, first // width)), ANY],
        out_specs=[pl.BlockSpec((tall, width), lambda i: (i, 0)), ANY],
        cost_estimate=FREE,
        compiler_params=params(),
    )(array, token)
    return out[1], out[0]


def activate(token, pre_act):
    rows, hidden = pre_act.shape
    tall, wide = divisor(rows, 512, 128), divisor(hidden, 512, 128)

    def kernel(x_ref, token_ref, out_ref, slopes_ref, token_out):
        value, slopes = gelu_pair(x_ref[...].astype(jnp.float32))
        out_ref[...] = value.T.astype(jnp.bfloat16)
        slopes_ref[...] = slopes

    tile = pl.BlockSpec((tall, wide), lambda j, i: (i, j))
    out = pl.pallas_call(
        kernel,
        out_shape=[
            jax.ShapeDtypeStruct((hidden, rows), jnp.bfloat16),
            jax.ShapeDtypeStruct((rows, hidden), jnp.float32),
            TOKEN,
        ],
        grid=(hidden // wide, rows // tall),
        in_specs=[tile, ANY],
        out_specs=[pl.BlockSpec((wide, tall), lambda j, i: (j, i)), tile, ANY],
        cost_estimate=FREE,
        compiler_params=params(),
    )(pre_act, token)
    return out[2], out[0], out[1]


def terms(token, table, base, pieces, acts, part, group, send, factor, with_rows):
    nc, rows, width = len(acts), acts[0].shape[1], pieces[0][0].shape[1]
    hidden = acts[0].shape[0]
    block = divisor(part, BLOCK if width <= 1024 else BLOCK // 2, 16)
    blocks = part // block
    steps = len(group) * blocks
    away = (len(group) - group.count(0)) * blocks
    own = group[-1] == 0
    strip = rows // steps if with_rows else 0

    def kernel(table_ref, *refs):
        refs = list(refs)
        piece_refs = [refs.pop(0) for _ in pieces]
        act_refs = [refs.pop(0) for _ in acts]
        refs.pop(0)
        if send is not None:
            refs.pop(0)
        send_ref = refs.pop(0) if away else None
        own_ref = refs.pop(0) if own else None
        row_outs = [refs.pop(0) for _ in range(nc if with_rows else 0)]
        refs.pop(0)
        held, sems = refs
        i = pl.program_id(0)

        @pl.when(i == 0)
        def _():
            copies = []
            for p, (_, first, count, place) in enumerate(pieces):
                to = pl.multiple_of(table_ref[place], 16)
                copies.append(
                    pltpu.make_async_copy(
                        piece_refs[p].at[pl.ds(first, count)], held.at[pl.ds(to, count)], sems.at[p]
                    )
                )
            for copy in copies:
                copy.start()
            for copy in copies:
                copy.wait()

        for j, ref in enumerate(row_outs):
            ref[...] = held[pl.ds(pl.multiple_of(j * rows + i * strip, 16), strip), :]
        total = None
        for j in range(nc):
            term = jnp.dot(
                act_refs[j][...],
                held[j * rows : (j + 1) * rows, :],
                preferred_element_type=jnp.float32,
            )
            total = term if total is None else total + term
        total = total * factor
        if away and own:

            @pl.when(i < away)
            def _():
                send_ref[...] = total.astype(send_ref.dtype)

            @pl.when(i >= away)
            def _():
                own_ref[...] = total

        elif own:
            own_ref[...] = total
        else:
            send_ref[...] = total.astype(send_ref.dtype)

    def act_map(i, table_ref):
        distance = group[0] - i // blocks
        return table_ref[base + distance] * blocks + i % blocks, 0

    def send_map(i, table_ref):
        return act_map(jnp.minimum(i, away - 1), table_ref)

    shapes, specs, aliases = [], [], {}
    operands = [p[0] for p in pieces] + list(acts) + [token]
    in_specs = [ANY] * len(pieces) + [pl.BlockSpec((block, rows), act_map)] * nc + [ANY]
    if send is not None:
        operands.append(send)
        in_specs.append(ANY)
        if away:
            aliases = {len(operands): 0}
    if away:
        shapes.append(jax.ShapeDtypeStruct((hidden, width), jnp.bfloat16))
        specs.append(pl.BlockSpec((block, width), send_map))
    if own:
        shapes.append(jax.ShapeDtypeStruct((part, width), jnp.float32))
        specs.append(
            pl.BlockSpec((block, width), lambda i, t: (jnp.clip(i - away, 0, blocks - 1), 0))
        )
    if with_rows:
        shapes += [jax.ShapeDtypeStruct((rows, width), jnp.bfloat16)] * nc
        specs += [pl.BlockSpec((strip, width), lambda i, t: (i, 0))] * nc
    out = list(
        pl.pallas_call(
            kernel,
            out_shape=shapes + [TOKEN],
            grid_spec=pltpu.PrefetchScalarGridSpec(
                num_scalar_prefetch=1,
                grid=(steps,),
                in_specs=in_specs,
                out_specs=specs + [ANY],
                scratch_shapes=[
                    pltpu.VMEM((nc * rows, width), jnp.bfloat16),
                    pltpu.SemaphoreType.DMA((len(pieces),)),
                ],
            ),
            input_output_aliases=aliases,
            cost_estimate=FREE,
            compiler_params=params(),
        )(table, *operands)
    )
    sent = out.pop(0) if away else send
    kept = out.pop(0) if own else None
    return out[-1], sent, kept, out[:-1]


def products(token, features, weights, spans, total, slopes):
    rows, hidden = features[0][0].shape[0], weights[0].shape[0]
    nc = len(weights)
    last = slopes is not None
    wide = nc * sum(width for width, _ in spans)
    tall = divisor(rows, 512 if wide <= 1024 else 256, 16)

    def kernel(*refs):
        refs = list(refs)
        lefts = [refs.pop(0) for _ in range(nc * len(spans))]
        rights = [refs.pop(0) for _ in range(nc * len(spans))]
        total_ref = refs.pop(0) if total is not None else None
        slopes_ref = refs.pop(0) if last else None
        out_ref = refs[1]
        value = None
        for left, right in zip(lefts, rights):
            term = lax.dot_general(
                left[...],
                right[...],
                (((1,), (1,)), ((), ())),
                preferred_element_type=jnp.float32,
            )
            value = term if value is None else value + term
        if total_ref is not None:
            value = value + total_ref[...]
        if last:
            value = value * slopes_ref[...]
        out_ref[...] = value.astype(out_ref.dtype)

    tile = pl.BlockSpec((tall, hidden), lambda i: (i, 0))
    operands, specs = [], []
    for ours, (width, _) in zip(features, spans):
        operands += ours
        specs += [pl.BlockSpec((tall, width), lambda i: (i, 0))] * nc
    for width, first in spans:
        operands += weights
        specs += [
            pl.BlockSpec(
                (hidden, width),
                lambda i, b=first // width: (0, b),
                pipeline_mode=pl.Buffered(1),
            )
        ] * nc
    aliases = {}
    if total is not None:
        if not last:
            aliases = {len(operands): 0}
        operands.append(total)
        specs.append(tile)
    if last:
        operands.append(slopes)
        specs.append(tile)
    kind = jnp.bfloat16 if last else jnp.float32
    out = pl.pallas_call(
        kernel,
        out_shape=[jax.ShapeDtypeStruct((rows, hidden), kind), TOKEN],
        grid=(rows // tall,),
        in_specs=specs + [ANY],
        out_specs=[tile, ANY],
        input_output_aliases=aliases,
        cost_estimate=FREE,
        compiler_params=params(),
    )(*operands, token)
    return out[1], out[0]


def add_up(token, table, base, own, arrived, whole, shape, span):
    width, first = span
    rows = shape[0]
    tall = divisor(rows, 384, 16)
    steps = rows // tall
    whole_blocks = len(arrived) == 1 and arrived[0].shape[0] > rows
    count = arrived[0].shape[0] // rows - 1 if whole_blocks else len(arrived)

    def kernel(table_ref, *refs):
        value = refs[0][...]
        for ref in refs[1 : 1 + count]:
            value = value + ref[...].astype(jnp.float32)
        refs[-2][...] = value

    def other(d):
        if not whole_blocks:
            return pl.BlockSpec((tall, width), lambda i, t: (i, 0))
        return pl.BlockSpec((tall, width), lambda i, t: (t[base + d] * steps + i, 0))

    operands = [own] + (arrived * count if whole_blocks else arrived)
    specs, aliases = [pl.BlockSpec((tall, width), lambda i, t: (i, 0))], {}
    specs += [other(d) for d in range(1, count + 1)]
    if whole is not None:
        aliases = {len(operands) + 1: 0}
        operands.append(whole)
        specs.append(ANY)
    out = pl.pallas_call(
        kernel,
        out_shape=[jax.ShapeDtypeStruct(shape, jnp.float32), TOKEN],
        grid_spec=pltpu.PrefetchScalarGridSpec(
            num_scalar_prefetch=1,
            grid=(steps,),
            in_specs=specs + [ANY],
            out_specs=[pl.BlockSpec((tall, width), lambda i, t: (i, first // width)), ANY],
        ),
        input_output_aliases=aliases,
        cost_estimate=FREE,
        compiler_params=params(),
    )(table, *operands, token)
    return out[1], out[0]


def on_device(n, nc, nr, pre_act, w_out, grad_out):
    tokens = grad_out.shape[0] * n * nr
    factor = float(tokens) ** (-0.5)
    row, col, rep = (lax.axis_index(axis) for axis in ("row", "col", "rep"))
    local = grad_out.shape[0]
    rows, hidden = pre_act.shape
    part = hidden // nr
    shape = (part, grad_out.shape[1])
    spans = stages_of(grad_out.shape[1])
    count = len(spans)
    groups = GROUPS if count == len(STAGES) else ((0,),)
    distances = list(range(nr - 1, -1, -1))

    def partner(d):
        return rep ^ d if nr & (nr - 1) == 0 else (rep + d) % nr

    places = [((j - col + nc) % nc) * rows for j in range(nc)]
    ring = n <= RING_LIMIT and n % nc == 0 and count > 1
    slots = [(row - s + 2 * n - col * (n // nc)) % n * local for s in range(n if ring else 0)]
    partners = [partner(d) for d in range(nr)]
    table = jnp.stack([jnp.int32(v) for v in places + partners + slots])
    token = jnp.zeros(TOKEN.shape, TOKEN.dtype)
    gathered, features, owns, arrived = {}, {}, {}, {}
    grad_act = grad_weight = None

    def gather(token, k):
        if k >= count:
            return token
        token, columns = cut(token, grad_out, *spans[k])
        gathered[k] = lax.all_gather(columns, "row", axis=0, tiled=True)
        return token

    def add_stage(token, k, whole):
        return add_up(token, table, nc, owns[k], arrived[k], whole, shape, spans[k])

    steps = []
    token = gather(token, 1 if ring else 0)
    if ring:
        token, columns = cut(token, grad_out, *spans[0])
        steps = [columns]
    token = gather(token, 2 if ring else 1)
    token, act, slopes = activate(token, pre_act)
    acts = [act] + [swap(act, "col", nc, nc - j) for j in range(1, nc)]
    weights = [w_out] + [swap(w_out, "col", nc, nc - j) for j in range(1, nc)]
    for s in range(1, n if ring else 0):
        piece = swap(steps[-1], "row", n, 1)
        if s < n - 1:
            token, piece = pass_on(token, piece)
        steps.append(piece)
    if not ring:
        token = gather(token, 2)

    for k in range(count):
        if 0 < k < count - LATE:
            token, grad_weight = add_stage(token, k - 1, grad_weight)
        if ring and k == 0:
            listed = [(steps[s], 0, local, nc + nr + s) for s in range(n)]
        else:
            listed = [(gathered[k], j * rows, rows, j) for j in range(nc)]
        token, sent, own, own_rows = terms(
            token, table, nc, listed, acts, part, distances, None, factor, True
        )
        features[k] = [own_rows[0]] + [swap(own_rows[j], "col", nc, j) for j in range(1, nc)]
        owns[k], arrived[k] = own, []
        if nr > 1 and k < max(1, count - PERMUTED):
            arrived[k] = [lax.all_to_all(sent, "rep", 0, 0, tiled=True)]
        elif nr > 1:
            arrived[k] = []
            for d in reversed(distances[:-1]):
                block = lax.dynamic_slice_in_dim(sent, partner(d) * part, part, 0)
                way = [(p, p ^ d if nr & (nr - 1) == 0 else (p + d) % nr) for p in range(nr)]
                arrived[k].append(lax.ppermute(block, "rep", way))
        token = gather(token, k + (2 if ring else 3)) if not ring or k > 0 else token
        for ks in groups:
            if ks[-1] == k:
                token, grad_act = products(
                    token,
                    [features[q] for q in ks],
                    weights,
                    [spans[q] for q in ks],
                    grad_act,
                    slopes if k == count - 1 else None,
                )
    for k in range(max(0, count - LATE - 1), count):
        token, grad_weight = add_stage(token, k, grad_weight)
    return grad_act, grad_weight


def solution(mesh):
    n, nc, nr = (mesh.shape[axis] for axis in ("row", "col", "rep"))
    in_specs = (P(("rep", "col"), "row"), P("row", "col"), P(("rep", "row"), "col"))
    out_specs = (P(("rep", "col"), "row"), P(("row", "rep"), "col"))
    return jax.shard_map(
        functools.partial(on_device, n, nc, nr),
        mesh=mesh,
        in_specs=in_specs,
        out_specs=out_specs,
        check_vma=False,
    )
```
